32 devices in a mesh: groups: 2 (over x), row: 16 (over z, y, core).
Axes of the slice: x: 2, y: 2, z: 4, core: 2. Of those that a mesh axis runs over, the one named last changes fastest.
Arguments:
- hblocks: float32 [1024, 6, 128, 128], P(('groups', 'row')), parts along dimension 0, may hold values from -0.21875 to 0.21875
- hcols: int32 [1024, 6], P(('groups', 'row')), parts along dimension 0, may hold values from 0 to 511, as said below
- hmask: int32 [1024, 6], P(('groups', 'row')), parts along dimension 0, may hold values 0 or 1
- tmask: int32 [1024, 2], P('groups'), parts along dimension 0, may hold values from 0 to 1, as said below
- owner: int32 [1024], P('groups'), parts along dimension 0, may hold values from 0 to 15, as said below
- cheb_now: float32 [131072, 256], P(('groups', 'row')), parts along dimension 0, may hold values from -6 to 6
- cheb_prev: float32 [131072, 256], P(('groups', 'row')), parts along dimension 0, may hold values from -6 to 6
Outputs:
- cheb_next: float32 [131072, 256], P(('groups', 'row')), parts along dimension 0
The draws below stay inside these ranges and needn't reach their ends.
There are 2 independent parts, one for each index of `groups`. The reference program is written for one: setup_inputs(seed, part) draws one part's arguments, and reference() takes and returns one part's arrays. A program takes and returns all parts, laid end to end along the dimension named above; each array names one. Nothing has to cross between parts.
Inputs may be any that keep to these rules, and one draw needn't show every extreme that they name: `hcols`: each block row names 6 different block columns, each within 64 block rows of its own in the periodic order. `tmask`: among the block rows of one device at most 32 blocks are occupied, exactly 32 on some device. The block rows of one device go to every owner exactly 2 at a time.
All inputs are finite; a program needn't handle non-finite values. No bound on the sum of `hmask` on one device may be relied on, other than what follows from the above.
Results may differ from the reference program's by a relative error of at most 0.00007.
Values sent between devices are 32-bit elements; how exact they have to be, the bound alone decides.
A program may use at most 192 MiB of HBM per device.

```python
import jax
import jax.numpy as jnp
from jax import lax

BLK = 128
RB = 32
NNZ = 6
WB = 2
REACH = 2
CAP = 2
NB = 512
W = 256
TOCC = 32


def draw_hcols(key, part):
    key = jax.random.fold_in(key, 11)
    span = 2 * REACH * RB + 1
    keys = jax.random.split(key, NB)
    perms = jax.vmap(lambda k: jax.random.permutation(k, span))(keys)[:, :NNZ]
    offsets = perms.astype(jnp.int32) - REACH * RB
    rows_idx = jnp.arange(NB, dtype=jnp.int32)[:, None]
    return ((rows_idx + offsets) % NB).astype(jnp.int32)


def draw_tmask(key, part):
    key = jax.random.fold_in(key, 12)
    devices_count = NB // RB
    slots = RB * WB
    key_count, key_full, key_perm = jax.random.split(key, 3)
    counts = jax.random.randint(key_count, (devices_count,), TOCC // 4, TOCC + 1)
    fullest = jax.random.randint(key_full, (), 0, devices_count)
    counts = jnp.where(jnp.arange(devices_count) == fullest, TOCC, counts)
    ranks = jax.vmap(lambda k: jax.random.permutation(k, slots))(jax.random.split(key_perm, devices_count))
    marks = (ranks < counts[:, None]).astype(jnp.int32)
    return marks.reshape(NB, WB)


def draw_owner(key, part):
    key = jax.random.fold_in(key, 13)
    devices_count = NB // RB
    key_base, key_turn = jax.random.split(key)
    base = jax.random.permutation(key_base, devices_count)[:RB // CAP].astype(jnp.int32)
    steps_to = jnp.repeat(base, CAP)
    turns = jax.random.randint(key_turn, (devices_count,), 0, RB)
    local = jnp.arange(RB, dtype=jnp.int32)
    source = jnp.arange(devices_count, dtype=jnp.int32)
    picked = steps_to[(local[None, :] + turns[:, None]) % RB]
    return ((source[:, None] + picked) % devices_count).reshape(NB).astype(jnp.int32)


def set_ends(array, key, low, high):
    shape = array.shape
    spot = [jax.random.randint(jax.random.fold_in(key, axis), (), 0, shape[axis]) for axis in range(len(shape))]
    array = array.at[tuple(spot)].set(low)
    longest = shape.index(max(shape))
    spot[longest] = (spot[longest] + 1) % shape[longest]
    return array.at[tuple(spot)].set(high)


def steps_of(own_key, shape, shards, low, largest):
    def one(dim, blocks):
        draws = jax.random.uniform(jax.random.fold_in(jax.random.fold_in(own_key, 6), dim), (blocks,), jnp.float32, low / len(shards), largest / len(shards))
        return jnp.repeat(jnp.exp(draws), shape[dim] // blocks).reshape((-1,) + (1,) * (len(shape) - dim - 1))

    factor_of = one(*shards[0])
    for cut in shards[1:]:
        factor_of = factor_of * one(*cut)
    return factor_of


def noise(rng, extent, spread, limit, shards=(), kind=jnp.bfloat16):
    result = spread * jax.random.normal(rng, extent, jnp.float32)
    if shards:
        result = result * steps_of(rng, extent, shards, -0.22, 0.18)
    return jnp.clip(result, -limit, limit).astype(kind)


def setup_inputs(seed: int = 0, part: int = 0) -> dict:
    seeds = jax.random.split(jax.random.key(seed), 8)
    part_keys = jax.random.split(jax.random.fold_in(seeds[7], part), 8)
    hblocks = noise(part_keys[0], (NB, NNZ, BLK, BLK), (NNZ * BLK) ** -0.5, 0.21875, ((0, 16),), jnp.float32)
    hcols = draw_hcols(jax.random.fold_in(jax.random.fold_in(seeds[7], part), 71), part)
    hmask = set_ends((jax.random.randint(part_keys[2], (NB, NNZ), 0, 4) < 3).astype(jnp.int32), jax.random.fold_in(part_keys[2], 1), 0, 1)
    tmask = draw_tmask(jax.random.fold_in(jax.random.fold_in(seeds[7], part), 71), part)
    owner = draw_owner(jax.random.fold_in(jax.random.fold_in(seeds[7], part), 71), part)
    cheb_now = noise(part_keys[5], (NB * BLK, W), 1.0, 6.0, ((0, 16),), jnp.float32)
    cheb_prev = noise(part_keys[6], (NB * BLK, W), 1.0, 6.0, ((0, 16),), jnp.float32)
    return dict(hblocks=hblocks, hcols=hcols, hmask=hmask, tmask=tmask, owner=owner, cheb_now=cheb_now, cheb_prev=cheb_prev)


def reference(hblocks, hcols, hmask, tmask, owner, cheb_now, cheb_prev):
    nblocks = hblocks.shape[0]
    width = cheb_now.shape[1]
    masked = cheb_now.reshape(nblocks, BLK, WB, BLK) * tmask[:, None, :, None].astype(jnp.float32)
    masked = masked.reshape(nblocks, BLK, width)
    weights = hblocks * hmask[:, :, None, None].astype(jnp.float32)
    groups_count = nblocks // RB

    def one_group(pair):
        weight, columns = pair
        picked = masked[columns]
        return jnp.einsum("rsij,rsjw->riw", weight, picked, precision=lax.Precision.HIGHEST)

    product = lax.map(one_group, (weights.reshape(groups_count, RB, NNZ, BLK, BLK), hcols.reshape(groups_count, RB, NNZ)))
    product = product.reshape(nblocks, BLK, width)
    fresh = 2.0 * product - cheb_prev.reshape(nblocks, BLK, width)
    ordering = jnp.argsort(owner, stable=True)
    return fresh[ordering].reshape(nblocks * BLK, width)
```

```python
import functools

import jax
import jax.numpy as jnp
from jax import lax
from jax.experimental import pallas as pl
from jax.experimental.pallas import tpu as pltpu
from jax.sharding import PartitionSpec as P

REACH = 2
WINDOW = 2 * REACH + 1
OCCUPIED = 32
CHUNKS = 8
MESH = pl.DeviceIdType.MESH


def remote(src, dst, send, recv, to):
    return pltpu.make_async_remote_copy(
        src_ref=src, dst_ref=dst, send_sem=send, recv_sem=recv,
        device_id={"row": to}, device_id_type=MESH,
    )


def halo_kernel(n, source_ref, slab_ref, win_ref, packed, near_s, near_r, far_s, far_r, sib_s, sib_r, fwd_s, fwd_r, own_sem):
    me = lax.axis_index("row")
    core = lax.rem(me, 2)
    odd = lax.rem(me // 2, 2)
    partner = me + 2 - 4 * odd
    relay_to = lax.rem(me + 4 - 8 * odd + n, n)
    relay_from = lax.rem(me - 4 + 8 * odd + n, n)
    sibling = me + 1 - 2 * core
    per = OCCUPIED // CHUNKS
    blk = slab_ref.shape[1]

    barrier = pltpu.get_barrier_semaphore()
    for other in (partner, relay_to, relay_from, sibling):
        pl.semaphore_signal(barrier, inc=1, device_id={"row": other}, device_id_type=MESH)
    pl.semaphore_wait(barrier, 4)

    def part(slot, i):
        return win_ref.at[slot, pl.ds(i * per, per)]

    def near(i):
        return remote(packed.at[pl.ds(i * per, per)], part(4 * odd, i), near_s.at[i], near_r.at[i], partner)

    def sib(i):
        return remote(packed.at[pl.ds(i * per, per)], part(1 + 2 * core, i), sib_s.at[i], sib_r.at[i], sibling)

    def far(i):
        return remote(part(4 - 4 * odd, i), part(4 * odd, i), far_s.at[i], far_r.at[i], relay_to)

    def fwd(i):
        return remote(part(4 - 4 * core, i), part(3 - 2 * core, i), fwd_s.at[i], fwd_r.at[i], sibling)

    def arrived(slot, i, sems):
        return remote(part(slot, i), part(slot, i), sems.at[i], sems.at[i], partner)

    def own(i):
        return pltpu.make_async_copy(packed.at[pl.ds(i * per, per)], part(REACH, i), own_sem.at[i])

    for i in range(CHUNKS):
        for j in range(per):
            spot = source_ref[i * per + j]
            rows = slab_ref[spot // 2]
            packed[i * per + j] = jnp.where(lax.rem(spot, 2) == 0, rows[:, :blk], rows[:, blk:])
        near(i).start()
    for i in range(CHUNKS):
        sib(i).start()
        own(i).start()

    for i in range(CHUNKS):
        arrived(4 - 4 * odd, i, near_r).wait_recv()
        far(i).start()

        @pl.when(odd == core)
        def _():
            fwd(i).start()

    for i in range(CHUNKS):
        arrived(4 * odd, i, far_r).wait_recv()

        @pl.when(odd != core)
        def _():
            fwd(i).start()

    for i in range(CHUNKS):
        arrived(3 - 2 * core, i, sib_r).wait_recv()
        arrived(1 + 2 * core, i, fwd_r).wait_recv()
        near(i).wait_send()
        sib(i).wait_send()
        far(i).wait_send()
        fwd(i).wait_send()
        own(i).wait()


def halo(source, slab, n):
    rb, blk, width = slab.shape
    sems = [pltpu.SemaphoreType.DMA((CHUNKS,)) for _ in range(9)]
    return pl.pallas_call(
        functools.partial(halo_kernel, n),
        out_shape=jax.ShapeDtypeStruct((WINDOW, OCCUPIED, blk, blk), jnp.float32),
        in_specs=[pl.BlockSpec(memory_space=pltpu.SMEM), pl.BlockSpec(memory_space=pltpu.VMEM)],
        out_specs=pl.BlockSpec(memory_space=pl.ANY),
        scratch_shapes=[pltpu.VMEM((OCCUPIED, blk, blk), jnp.float32)] + sems,
        compiler_params=pltpu.CompilerParams(collective_id=0, has_side_effects=True, vmem_limit_bytes=32 << 20),
    )(source, slab)


def term_kernel(table_ref, column_ref, place_ref, win_ref, blocks_ref, prev_ref, out_ref, high, low):
    del place_ref
    row = pl.program_id(0)
    slots = blocks_ref.shape[1]
    count = win_ref.shape[0]

    @pl.when(row == 0)
    def _():
        @pl.loop(0, count)
        def _(i):
            x = win_ref[i]
            h = x.astype(jnp.bfloat16)
            high[i] = h
            low[i] = (x - h.astype(jnp.float32)).astype(jnp.bfloat16)

        high[count] = jnp.zeros(high.shape[1:], high.dtype)
        low[count] = jnp.zeros(low.shape[1:], low.dtype)

    total = None
    for pair in range(0, slots, 2):
        a_high, a_low, b_high, b_low = [], [], [], []
        for s in range(pair, min(pair + 2, slots)):
            a = blocks_ref[0, s]
            h = a.astype(jnp.bfloat16)
            a_high.append(h)
            a_low.append((a - h.astype(jnp.float32)).astype(jnp.bfloat16))
            column = column_ref[row * slots + s]
            left, right = table_ref[2 * column], table_ref[2 * column + 1]
            b_high.append(jnp.concatenate([high[left], high[right]], axis=1))
            b_low.append(jnp.concatenate([low[left], low[right]], axis=1))
        a_high, a_low = jnp.concatenate(a_high, axis=1), jnp.concatenate(a_low, axis=1)
        b_high, b_low = jnp.concatenate(b_high, axis=0), jnp.concatenate(b_low, axis=0)
        both = jnp.dot(jnp.concatenate([a_high, a_low], axis=0), b_high, preferred_element_type=jnp.float32)
        rows = a_high.shape[0]
        piece = both[:rows] + both[rows:] + jnp.dot(a_high, b_low, preferred_element_type=jnp.float32)
        total = piece if total is None else total + piece
    out_ref[0] = 2.0 * total - prev_ref[0]


def term(table, column, place, win, blocks, prev):
    rb, slots, blk, _ = blocks.shape
    width = prev.shape[2]
    count = win.shape[0]
    return pl.pallas_call(
        term_kernel,
        out_shape=jax.ShapeDtypeStruct((rb, blk, width), jnp.float32),
        grid_spec=pltpu.PrefetchScalarGridSpec(
            num_scalar_prefetch=3,
            grid=(rb,),
            in_specs=[
                pl.BlockSpec(memory_space=pltpu.VMEM),
                pl.BlockSpec((1, slots, blk, blk), lambda i, t, c, p: (i, 0, 0, 0)),
                pl.BlockSpec((1, blk, width), lambda i, t, c, p: (i, 0, 0)),
            ],
            out_specs=pl.BlockSpec((1, blk, width), lambda i, t, c, p: (p[i], 0, 0)),
            scratch_shapes=[pltpu.VMEM((count + 1, blk, blk), jnp.bfloat16)] * 2,
        ),
        compiler_params=pltpu.CompilerParams(vmem_limit_bytes=48 << 20),
    )(table, column, place, win, blocks, prev)


def exchange_kernel(n, send_ref, out_ref, send_sem, recv_sem, own_sem):
    me = lax.axis_index("row")
    per = send_ref.shape[0] // n
    barrier = pltpu.get_barrier_semaphore()

    @pl.loop(1, n)
    def _(j):
        pl.semaphore_signal(barrier, inc=1, device_id={"row": lax.rem(me + j, n)}, device_id_type=MESH)

    pl.semaphore_wait(barrier, n - 1)

    def copy(j):
        to = lax.rem(me + j, n)
        return remote(
            send_ref.at[pl.ds(to * per, per)], out_ref.at[pl.ds(me * per, per)],
            send_sem.at[j], recv_sem.at[j], to,
        )

    def arrival(j):
        came = lax.rem(me + n - j, n)
        piece = out_ref.at[pl.ds(came * per, per)]
        return remote(piece, piece, send_sem.at[j], recv_sem.at[j], came)

    @pl.loop(1, n)
    def _(j):
        copy(lax.rem(j + n // 2 - 1, n - 1) + 1).start()

    own = pltpu.make_async_copy(
        send_ref.at[pl.ds(me * per, per)], out_ref.at[pl.ds(me * per, per)], own_sem
    )
    own.start()
    own.wait()

    @pl.loop(1, n)
    def _(j):
        copy(j).wait_send()
        arrival(j).wait_recv()


def exchange(send, n):
    return pl.pallas_call(
        functools.partial(exchange_kernel, n),
        out_shape=jax.ShapeDtypeStruct(send.shape, send.dtype),
        in_specs=[pl.BlockSpec(memory_space=pl.ANY)],
        out_specs=pl.BlockSpec(memory_space=pl.ANY),
        scratch_shapes=[
            pltpu.SemaphoreType.DMA((n,)),
            pltpu.SemaphoreType.DMA((n,)),
            pltpu.SemaphoreType.DMA,
        ],
        compiler_params=pltpu.CompilerParams(collective_id=1, has_side_effects=True),
    )(send)


def local(hblocks, hcols, hmask, tmask, owner, cheb_now, cheb_prev):
    n = lax.axis_size("row")
    me = lax.axis_index("row")
    rb, slots, blk, _ = hblocks.shape
    width = cheb_now.shape[1]
    wb = width // blk
    nblocks = rb * n
    per_owner = rb // n
    cells = rb * wb
    zero = WINDOW * OCCUPIED

    iota = jnp.arange(cells, dtype=jnp.int32)
    near = (me - REACH + jnp.arange(WINDOW, dtype=jnp.int32)) % n
    marks = jnp.take(tmask.reshape(n, cells), near, axis=0)
    ahead = (iota[:, None] < iota[None, :]).astype(jnp.int32)
    spot = jnp.sum(marks[:, :, None] * ahead[None], axis=1)
    table = jnp.where(marks == 1, jnp.arange(WINDOW, dtype=jnp.int32)[:, None] * OCCUPIED + spot, zero)
    table = jnp.concatenate([table.reshape(-1), jnp.full((wb,), zero, jnp.int32)])
    hit = (spot[REACH][None, :] == jnp.arange(OCCUPIED, dtype=jnp.int32)[:, None]) & (marks[REACH][None, :] == 1)
    source = jnp.sum(jnp.where(hit, iota[None, :], 0), axis=1)

    relative = (hcols - (me - REACH) * rb) % nblocks
    column = jnp.where(hmask == 1, relative, WINDOW * rb).reshape(-1)

    my_owner = lax.dynamic_slice_in_dim(owner, me * rb, rb, 0)
    row = jnp.arange(rb, dtype=jnp.int32)
    earlier = (my_owner[:, None] == my_owner[None, :]) & (row[None, :] < row[:, None])
    place = my_owner * per_owner + jnp.sum(earlier.astype(jnp.int32), axis=1)

    win = halo(source, cheb_now.reshape(rb, blk, width), n)
    send = term(
        table, column, place, win.reshape(zero, blk, blk), hblocks, cheb_prev.reshape(rb, blk, width)
    )
    return exchange(send, n).reshape(rb * blk, width)


def solution(mesh):
    in_specs = (
        P(("groups", "row"), None, None, None),
        P(("groups", "row"), None),
        P(("groups", "row"), None),
        P("groups", None),
        P("groups"),
        P(("groups", "row"), None),
        P(("groups", "row"), None),
    )
    out_specs = P(("groups", "row"), None)
    return jax.shard_map(local, mesh=mesh, in_specs=in_specs, out_specs=out_specs, check_vma=False)
```

```python
import functools

import jax
import jax.numpy as jnp
from jax import lax
from jax.experimental import pallas as pl
from jax.experimental.pallas import tpu as pltpu
from jax.sharding import PartitionSpec as P

REACH = 2
WINDOW = 2 * REACH + 1
OCCUPIED = 32
CHUNKS = 16
MESH = pl.DeviceIdType.MESH


def remote(src, dst, send, recv, to):
    return pltpu.make_async_remote_copy(
        src_ref=src, dst_ref=dst, send_sem=send, recv_sem=recv,
        device_id={"row": to}, device_id_type=MESH,
    )


def partner_of(me, m, n):
    if n & (n - 1):
        return lax.rem(me + m, n), lax.rem(me + n - m, n)
    to = me
    bit = 1
    while bit < n:
        to = to + lax.rem(m // bit, 2) * (bit - 2 * bit * lax.rem(me // bit, 2))
        bit *= 2
    return to, to


def split(x):
    high = x.astype(jnp.bfloat16)
    return high, (x - high.astype(jnp.float32)).astype(jnp.bfloat16)


def term_kernel(
    n, source_ref, table_ref, column_ref, inverse_ref, slab_hbm, blocks_hbm, prev_hbm, out_ref,
    slab, blocks, prev, packed, win, high, low, stage,
    near_s, near_r, far_s, far_r, sib_s, sib_r, fwd_s, fwd_r, send_sem, recv_sem, load_sem,
):
    me = lax.axis_index("row")
    core = lax.rem(me, 2)
    odd = lax.rem(me // 2, 2)
    partner = me + 2 - 4 * odd
    relay_to = lax.rem(me + 4 - 8 * odd + n, n)
    sibling = me + 1 - 2 * core
    chunk = OCCUPIED // CHUNKS
    rb, slots, blk, _ = blocks.shape
    per = rb // n
    zero = WINDOW * OCCUPIED

    slab_load = pltpu.make_async_copy(slab_hbm, slab, load_sem.at[0])
    blocks_load = pltpu.make_async_copy(blocks_hbm, blocks, load_sem.at[1])
    prev_load = pltpu.make_async_copy(prev_hbm, prev, load_sem.at[2])
    slab_load.start()

    barrier = pltpu.get_barrier_semaphore()

    @pl.loop(1, n)
    def _(j):
        pl.semaphore_signal(barrier, inc=1, device_id={"row": lax.rem(me + j, n)}, device_id_type=MESH)

    slab_load.wait()
    blocks_load.start()
    prev_load.start()
    pl.semaphore_wait(barrier, n - 1)

    def piece(i):
        return packed.at[pl.ds(i * chunk, chunk)]

    def part(slot, i):
        return win.at[pl.ds(slot * OCCUPIED + i * chunk, chunk)]

    def near(i):
        return remote(piece(i), part(4 * odd, i), near_s.at[i], near_r.at[i], partner)

    def sib(i):
        return remote(piece(i), part(1 + 2 * core, i), sib_s.at[i], sib_r.at[i], sibling)

    def far(i):
        return remote(part(4 - 4 * odd, i), part(4 * odd, i), far_s.at[i], far_r.at[i], relay_to)

    def fwd(i):
        return remote(part(4 - 4 * core, i), part(3 - 2 * core, i), fwd_s.at[i], fwd_r.at[i], sibling)

    def arrived(slot, i, sems):
        return remote(part(slot, i), part(slot, i), sems.at[i], sems.at[i], partner)

    def halve(slot, i):
        for k in range(chunk):
            at = slot * OCCUPIED + i * chunk + k
            high[at], low[at] = split(win[at])

    @pl.loop(0, CHUNKS)
    def _(i):
        for k in range(chunk):
            spot = source_ref[i * chunk + k]
            rows = slab[spot // 2]
            packed[i * chunk + k] = jnp.where(lax.rem(spot, 2) == 0, rows[:, :blk], rows[:, blk:])
        near(i).start()

    @pl.loop(0, CHUNKS)
    def _(i):
        sib(i).start()
        for k in range(chunk):
            at = i * chunk + k
            high[REACH * OCCUPIED + at], low[REACH * OCCUPIED + at] = split(packed[at])

    high[zero] = jnp.zeros((blk, blk), jnp.bfloat16)
    low[zero] = jnp.zeros((blk, blk), jnp.bfloat16)

    @pl.loop(0, CHUNKS)
    def _(i):
        arrived(4 - 4 * odd, i, near_r).wait_recv()
        far(i).start()

        @pl.when(odd == core)
        def _():
            fwd(i).start()

        halve(4 - 4 * odd, i)
        arrived(3 - 2 * core, i, sib_r).wait_recv()
        halve(3 - 2 * core, i)

    @pl.loop(0, CHUNKS)
    def _(i):
        arrived(4 * odd, i, far_r).wait_recv()

        @pl.when(odd != core)
        def _():
            fwd(i).start()

        halve(4 * odd, i)

    blocks_load.wait()
    prev_load.wait()

    @pl.loop(0, CHUNKS)
    def _(i):
        arrived(1 + 2 * core, i, fwd_r).wait_recv()
        halve(1 + 2 * core, i)

    def copy(m):
        to, _ = partner_of(me, m, n)
        return remote(
            stage.at[pl.ds(m * per, per)], out_ref.at[pl.ds(me * per, per)],
            send_sem.at[m], recv_sem.at[m], to,
        )

    def arrival(m):
        _, came = partner_of(me, m, n)
        rows = out_ref.at[pl.ds(came * per, per)]
        return remote(rows, rows, send_sem.at[m], recv_sem.at[m], came)

    def compute(m, r):
        to, _ = partner_of(me, m, n)
        row = inverse_ref[to * per + r]
        total = None
        for pair in range(0, slots, 2):
            a_high, a_low, b_high, b_low = [], [], [], []
            for s in range(pair, min(pair + 2, slots)):
                h, l = split(blocks[row, s])
                a_high.append(h)
                a_low.append(l)
                column = column_ref[row * slots + s]
                left, right = table_ref[2 * column], table_ref[2 * column + 1]
                b_high.append(jnp.concatenate([high[left], high[right]], axis=1))
                b_low.append(jnp.concatenate([low[left], low[right]], axis=1))
            a_high, a_low = jnp.concatenate(a_high, axis=1), jnp.concatenate(a_low, axis=1)
            b_high, b_low = jnp.concatenate(b_high, axis=0), jnp.concatenate(b_low, axis=0)
            both = jnp.dot(jnp.concatenate([a_high, a_low], axis=0), b_high, preferred_element_type=jnp.float32)
            add = both[:blk] + both[blk:] + jnp.dot(a_high, b_low, preferred_element_type=jnp.float32)
            total = add if total is None else total + add
        stage[m * per + r] = 2.0 * total - prev[row]

    @pl.loop(0, n - 1)
    def _(j):
        m = n - 1 - j
        @pl.loop(0, per)
        def _(r):
            compute(m, r)

        copy(m).start()

    @pl.loop(0, per)
    def _(r):
        compute(0, r)

    own = pltpu.make_async_copy(stage.at[pl.ds(0, per)], out_ref.at[pl.ds(me * per, per)], load_sem.at[3])
    own.start()

    @pl.loop(0, CHUNKS)
    def _(i):
        near(i).wait_send()
        sib(i).wait_send()
        far(i).wait_send()
        fwd(i).wait_send()

    own.wait()

    @pl.loop(0, n - 1)
    def _(j):
        m = n - 1 - j
        copy(m).wait_send()
        arrival(m).wait_recv()


def term(source, table, column, inverse, slab, blocks, prev, n):
    rb, _, blk, _ = blocks.shape
    width = prev.shape[2]
    count = WINDOW * OCCUPIED
    smem = pl.BlockSpec(memory_space=pltpu.SMEM)
    hbm = pl.BlockSpec(memory_space=pl.ANY)
    return pl.pallas_call(
        functools.partial(term_kernel, n),
        out_shape=jax.ShapeDtypeStruct((rb, blk, width), jnp.float32),
        in_specs=[smem] * 4 + [hbm] * 3,
        out_specs=hbm,
        scratch_shapes=[
            pltpu.VMEM(slab.shape, jnp.float32),
            pltpu.VMEM(blocks.shape, jnp.float32),
            pltpu.VMEM(prev.shape, jnp.float32),
            pltpu.VMEM((OCCUPIED, blk, blk), jnp.float32),
            pltpu.VMEM((count, blk, blk), jnp.float32),
            pltpu.VMEM((count + 1, blk, blk), jnp.bfloat16),
            pltpu.VMEM((count + 1, blk, blk), jnp.bfloat16),
            pltpu.VMEM(prev.shape, jnp.float32),
        ]
        + [pltpu.SemaphoreType.DMA((CHUNKS,)) for _ in range(8)]
        + [pltpu.SemaphoreType.DMA((n,))] * 2
        + [pltpu.SemaphoreType.DMA((4,))],
        compiler_params=pltpu.CompilerParams(collective_id=0, has_side_effects=True, vmem_limit_bytes=56 << 20),
    )(source, table, column, inverse, slab, blocks, prev)


def local(hblocks, hcols, hmask, tmask, owner, cheb_now, cheb_prev):
    n = lax.axis_size("row")
    me = lax.axis_index("row")
    rb, slots, blk, _ = hblocks.shape
    width = cheb_now.shape[1]
    wb = width // blk
    nblocks = rb * n
    per_owner = rb // n
    cells = rb * wb
    zero = WINDOW * OCCUPIED

    iota = jnp.arange(cells, dtype=jnp.int32)
    near = (me - REACH + jnp.arange(WINDOW, dtype=jnp.int32)) % n
    marks = jnp.take(tmask.reshape(n, cells), near, axis=0)
    ahead = (iota[:, None] < iota[None, :]).astype(jnp.int32)
    spot = jnp.sum(marks[:, :, None] * ahead[None], axis=1)
    table = jnp.where(marks == 1, jnp.arange(WINDOW, dtype=jnp.int32)[:, None] * OCCUPIED + spot, zero)
    table = jnp.concatenate([table.reshape(-1), jnp.full((wb,), zero, jnp.int32)])
    hit = (spot[REACH][None, :] == jnp.arange(OCCUPIED, dtype=jnp.int32)[:, None]) & (marks[REACH][None, :] == 1)
    source = jnp.sum(jnp.where(hit, iota[None, :], 0), axis=1)

    relative = (hcols - (me - REACH) * rb) % nblocks
    column = jnp.where(hmask == 1, relative, WINDOW * rb).reshape(-1)

    my_owner = lax.dynamic_slice_in_dim(owner, me * rb, rb, 0)
    row = jnp.arange(rb, dtype=jnp.int32)
    earlier = (my_owner[:, None] == my_owner[None, :]) & (row[None, :] < row[:, None])
    place = my_owner * per_owner + jnp.sum(earlier.astype(jnp.int32), axis=1)

    inverse = jnp.sum(jnp.where(place[None, :] == row[:, None], row[None, :], 0), axis=1)

    out = term(
        source, table, column, inverse,
        cheb_now.reshape(rb, blk, width), hblocks, cheb_prev.reshape(rb, blk, width), n,
    )
    return out.reshape(rb * blk, width)


def solution(mesh):
    in_specs = (
        P(("groups", "row"), None, None, None),
        P(("groups", "row"), None),
        P(("groups", "row"), None),
        P("groups", None),
        P("groups"),
        P(("groups", "row"), None),
        P(("groups", "row"), None),
    )
    out_specs = P(("groups", "row"), None)
    return jax.shard_map(local, mesh=mesh, in_specs=in_specs, out_specs=out_specs, check_vma=False)
```

```python
import functools

import jax
import jax.numpy as jnp
from jax import lax
from jax.experimental import pallas as pl
from jax.experimental.pallas import tpu as pltpu
from jax.sharding import PartitionSpec as P

REACH = 2
WINDOW = 2 * REACH + 1
OCCUPIED = 32
CHUNKS = 16
MESH = pl.DeviceIdType.MESH


def remote(src, dst, send, recv, to):
    return pltpu.make_async_remote_copy(
        src_ref=src, dst_ref=dst, send_sem=send, recv_sem=recv,
        device_id={"row": to}, device_id_type=MESH,
    )


def partner_of(me, m, n):
    if n & (n - 1):
        return lax.rem(me + m, n), lax.rem(me + n - m, n)
    to = me
    bit = 1
    while bit < n:
        to = to + lax.rem(m // bit, 2) * (bit - 2 * bit * lax.rem(me // bit, 2))
        bit *= 2
    return to, to


def split(x):
    high = x.astype(jnp.bfloat16)
    return high, (x - high.astype(jnp.float32)).astype(jnp.bfloat16)


def term_kernel(
    n, marks_ref, column_ref, owner_ref, slab_hbm, blocks_hbm, prev_hbm, out_ref,
    slab, blocks, prev, packed, win, high, low, stage, table_ref,
    near_s, near_r, far_s, far_r, sib_s, sib_r, fwd_s, fwd_r, send_sem, recv_sem, load_sem,
):
    me = lax.axis_index("row")
    core = lax.rem(me, 2)
    odd = lax.rem(me // 2, 2)
    partner = me + 2 - 4 * odd
    relay_to = lax.rem(me + 4 - 8 * odd + n, n)
    sibling = me + 1 - 2 * core
    chunk = OCCUPIED // CHUNKS
    rb, slots, blk, _ = blocks.shape
    per = rb // n
    zero = WINDOW * OCCUPIED
    wb = slab.shape[2] // blk
    span = WINDOW * rb + 1

    slab_load = pltpu.make_async_copy(slab_hbm, slab, load_sem.at[0])
    blocks_load = pltpu.make_async_copy(blocks_hbm, blocks, load_sem.at[1])
    prev_load = pltpu.make_async_copy(prev_hbm, prev, load_sem.at[2])
    slab_load.start()

    barrier = pltpu.get_barrier_semaphore()

    @pl.loop(1, n)
    def _(j):
        pl.semaphore_signal(barrier, inc=1, device_id={"row": lax.rem(me + j, n)}, device_id_type=MESH)

    slab_load.wait()
    blocks_load.start()
    prev_load.start()
    pl.semaphore_wait(barrier, n - 1)

    def piece(i):
        return packed.at[pl.ds(i * chunk, chunk)]

    def part(slot, i):
        return win.at[pl.ds(slot * OCCUPIED + i * chunk, chunk)]

    def near(i):
        return remote(piece(i), part(4 * odd, i), near_s.at[i], near_r.at[i], partner)

    def sib(i):
        return remote(piece(i), part(1 + 2 * core, i), sib_s.at[i], sib_r.at[i], sibling)

    def far(i):
        return remote(part(4 - 4 * odd, i), part(4 * odd, i), far_s.at[i], far_r.at[i], relay_to)

    def fwd(i):
        return remote(part(4 - 4 * core, i), part(3 - 2 * core, i), fwd_s.at[i], fwd_r.at[i], sibling)

    def arrived(slot, i, sems):
        return remote(part(slot, i), part(slot, i), sems.at[i], sems.at[i], partner)

    def halve(slot, i):
        for k in range(chunk):
            at = slot * OCCUPIED + i * chunk + k
            high[at], low[at] = split(win[at])

    def mark(device, c, r):
        return marks_ref[c * n * rb + device * rb + r]

    def occupied(which):
        seen, spot = 0, 0
        for c in range(wb):
            for r in range(rb):
                hit = mark(me, c, r)
                spot = jnp.where((hit == 1) & (seen == which), c * rb + r, spot)
                seen = seen + hit
        return spot

    def owned(to, rank):
        seen, row = 0, 0
        for b in range(rb):
            hit = owner_ref[me * rb + b] == to
            row = jnp.where(hit & (seen == rank), b, row)
            seen = seen + hit.astype(jnp.int32)
        return row

    @pl.loop(0, CHUNKS)
    def _(i):
        for k in range(chunk):
            spot = occupied(i * chunk + k)
            rows = slab[lax.rem(spot, rb)]
            packed[i * chunk + k] = jnp.where(spot < rb, rows[:, :blk], rows[:, blk:])
        near(i).start()

    @pl.loop(0, CHUNKS)
    def _(i):
        sib(i).start()
        for k in range(chunk):
            at = i * chunk + k
            high[REACH * OCCUPIED + at], low[REACH * OCCUPIED + at] = split(packed[at])

    high[zero] = jnp.zeros((blk, blk), jnp.bfloat16)
    low[zero] = jnp.zeros((blk, blk), jnp.bfloat16)

    @pl.loop(0, WINDOW)
    def _(w):
        device = lax.rem(me + w - REACH + n, n)

        seen = 0
        for c in range(wb):
            for r in range(rb):
                hit = mark(device, c, r)
                table_ref[c * span + w * rb + r] = jnp.where(hit == 1, w * OCCUPIED + seen, zero)
                seen = seen + hit

    for c in range(wb):
        table_ref[c * span + WINDOW * rb] = zero

    @pl.loop(0, CHUNKS)
    def _(i):
        arrived(4 - 4 * odd, i, near_r).wait_recv()
        far(i).start()

        @pl.when(odd == core)
        def _():
            fwd(i).start()

        halve(4 - 4 * odd, i)
        arrived(3 - 2 * core, i, sib_r).wait_recv()
        halve(3 - 2 * core, i)

    @pl.loop(0, CHUNKS)
    def _(i):
        arrived(4 * odd, i, far_r).wait_recv()

        @pl.when(odd != core)
        def _():
            fwd(i).start()

        halve(4 * odd, i)

    blocks_load.wait()
    prev_load.wait()

    @pl.loop(0, CHUNKS)
    def _(i):
        arrived(1 + 2 * core, i, fwd_r).wait_recv()
        halve(1 + 2 * core, i)

    def copy(m):
        to, _ = partner_of(me, m, n)
        return remote(
            stage.at[pl.ds(m * per, per)], out_ref.at[pl.ds(me * per, per)],
            send_sem.at[m], recv_sem.at[m], to,
        )

    def arrival(m):
        _, came = partner_of(me, m, n)
        rows = out_ref.at[pl.ds(came * per, per)]
        return remote(rows, rows, send_sem.at[m], recv_sem.at[m], came)

    def compute(m, r):
        to, _ = partner_of(me, m, n)
        row = owned(to, r)
        total = None
        for pair in range(0, slots, 2):
            a_high, a_low, b_high, b_low = [], [], [], []
            for s in range(pair, min(pair + 2, slots)):
                h, l = split(blocks[row, s])
                a_high.append(h)
                a_low.append(l)
                column = column_ref[s * rb + row]
                left, right = table_ref[column], table_ref[span + column]
                b_high.append(jnp.concatenate([high[left], high[right]], axis=1))
                b_low.append(jnp.concatenate([low[left], low[right]], axis=1))
            a_high, a_low = jnp.concatenate(a_high, axis=1), jnp.concatenate(a_low, axis=1)
            b_high, b_low = jnp.concatenate(b_high, axis=0), jnp.concatenate(b_low, axis=0)
            both = jnp.dot(jnp.concatenate([a_high, a_low], axis=0), b_high, preferred_element_type=jnp.float32)
            add = both[:blk] + both[blk:] + jnp.dot(a_high, b_low, preferred_element_type=jnp.float32)
            total = add if total is None else total + add
        stage[m * per + r] = 2.0 * total - prev[row]

    @pl.loop(0, n - 1)
    def _(j):
        m = n - 1 - j
        @pl.loop(0, per)
        def _(r):
            compute(m, r)

        copy(m).start()

    @pl.loop(0, per)
    def _(r):
        compute(0, r)

    own = pltpu.make_async_copy(stage.at[pl.ds(0, per)], out_ref.at[pl.ds(me * per, per)], load_sem.at[3])
    own.start()

    @pl.loop(0, CHUNKS)
    def _(i):
        near(i).wait_send()
        sib(i).wait_send()
        far(i).wait_send()
        fwd(i).wait_send()

    own.wait()

    @pl.loop(0, n - 1)
    def _(j):
        m = n - 1 - j
        copy(m).wait_send()
        arrival(m).wait_recv()


def term(marks, column, owner, slab, blocks, prev, n):
    rb, _, blk, _ = blocks.shape
    width = prev.shape[2]
    count = WINDOW * OCCUPIED
    smem = pl.BlockSpec(memory_space=pltpu.SMEM)
    hbm = pl.BlockSpec(memory_space=pl.ANY)
    return pl.pallas_call(
        functools.partial(term_kernel, n),
        out_shape=jax.ShapeDtypeStruct((rb, blk, width), jnp.float32),
        in_specs=[smem] * 3 + [hbm] * 3,
        out_specs=hbm,
        scratch_shapes=[
            pltpu.VMEM(slab.shape, jnp.float32),
            pltpu.VMEM(blocks.shape, jnp.float32),
            pltpu.VMEM(prev.shape, jnp.float32),
            pltpu.VMEM((OCCUPIED, blk, blk), jnp.float32),
            pltpu.VMEM((count, blk, blk), jnp.float32),
            pltpu.VMEM((count + 1, blk, blk), jnp.bfloat16),
            pltpu.VMEM((count + 1, blk, blk), jnp.bfloat16),
            pltpu.VMEM(prev.shape, jnp.float32),
            pltpu.SMEM((width // blk * (WINDOW * rb + 1),), jnp.int32),
        ]
        + [pltpu.SemaphoreType.DMA((CHUNKS,)) for _ in range(8)]
        + [pltpu.SemaphoreType.DMA((n,))] * 2
        + [pltpu.SemaphoreType.DMA((4,))],
        compiler_params=pltpu.CompilerParams(collective_id=0, has_side_effects=True, vmem_limit_bytes=49 << 20),
    )(marks, column, owner, slab, blocks, prev)


def local(hblocks, hcols, hmask, tmask, owner, cheb_now, cheb_prev):
    n = lax.axis_size("row")
    me = lax.axis_index("row")
    rb, slots, blk, _ = hblocks.shape
    width = cheb_now.shape[1]
    relative = (hcols - (me - REACH) * rb) % (rb * n)
    column = jnp.where(hmask == 1, relative, WINDOW * rb).T.reshape(-1)
    out = term(
        tmask.T.reshape(-1), column, owner,
        cheb_now.reshape(rb, blk, width), hblocks, cheb_prev.reshape(rb, blk, width), n,
    )
    return out.reshape(rb * blk, width)


def solution(mesh):
    in_specs = (
        P(("groups", "row"), None, None, None),
        P(("groups", "row"), None),
        P(("groups", "row"), None),
        P("groups", None),
        P("groups"),
        P(("groups", "row"), None),
        P(("groups", "row"), None),
    )
    out_specs = P(("groups", "row"), None)
    return jax.shard_map(local, mesh=mesh, in_specs=in_specs, out_specs=out_specs, check_vma=False)
```

```python
import functools

import jax
import jax.numpy as jnp
from jax import lax
from jax.experimental import pallas as pl
from jax.experimental.pallas import tpu as pltpu
from jax.sharding import PartitionSpec as P

REACH = 2
WINDOW = 2 * REACH + 1
OCCUPIED = 32
CHUNKS = 16
MESH = pl.DeviceIdType.MESH


def remote(src, dst, send, recv, to):
    return pltpu.make_async_remote_copy(
        src_ref=src, dst_ref=dst, send_sem=send, recv_sem=recv,
        device_id={"row": to}, device_id_type=MESH,
    )


def partner_of(me, m, n):
    if n & (n - 1):
        return lax.rem(me + m, n), lax.rem(me + n - m, n)
    to = me
    bit = 1
    while bit < n:
        to = to + lax.rem(m // bit, 2) * (bit - 2 * bit * lax.rem(me // bit, 2))
        bit *= 2
    return to, to


def split(x):
    high = x.astype(jnp.bfloat16)
    return high, (x - high.astype(jnp.float32)).astype(jnp.bfloat16)


def term_kernel(
    n, marks_ref, column_ref, owner_ref, slab_hbm, blocks_hbm, prev_hbm, out_ref,
    slab, blocks, prev, packed, win, high, low, stage, table_ref,
    near_s, near_r, far_s, far_r, sib_s, sib_r, fwd_s, fwd_r, send_sem, recv_sem, load_sem,
):
    me = lax.axis_index("row")
    core = lax.rem(me, 2)
    odd = lax.rem(me // 2, 2)
    partner = me + 2 - 4 * odd
    relay_to = lax.rem(me + 4 - 8 * odd + n, n)
    sibling = me + 1 - 2 * core
    chunk = OCCUPIED // CHUNKS
    rb, slots, blk, _ = blocks.shape
    per = rb // n
    zero = WINDOW * OCCUPIED
    wb = slab.shape[2] // blk
    span = WINDOW * rb + 1

    slab_load = pltpu.make_async_copy(slab_hbm, slab, load_sem.at[0])
    blocks_load = pltpu.make_async_copy(blocks_hbm, blocks, load_sem.at[1])
    prev_load = pltpu.make_async_copy(prev_hbm, prev, load_sem.at[2])
    slab_load.start()

    barrier = pltpu.get_barrier_semaphore()

    @pl.loop(1, n)
    def _(j):
        pl.semaphore_signal(barrier, inc=1, device_id={"row": lax.rem(me + j, n)}, device_id_type=MESH)

    slab_load.wait()
    blocks_load.start()
    prev_load.start()
    pl.semaphore_wait(barrier, n - 1)

    def piece(i):
        return packed.at[pl.ds(i * chunk, chunk)]

    def part(slot, i):
        return win.at[pl.ds(slot * OCCUPIED + i * chunk, chunk)]

    def near(i):
        return remote(piece(i), part(4 * odd, i), near_s.at[i], near_r.at[i], partner)

    def sib(i):
        return remote(piece(i), part(1 + 2 * core, i), sib_s.at[i], sib_r.at[i], sibling)

    def far(i):
        return remote(part(4 - 4 * odd, i), part(4 * odd, i), far_s.at[i], far_r.at[i], relay_to)

    def fwd(i):
        return remote(part(4 - 4 * core, i), part(3 - 2 * core, i), fwd_s.at[i], fwd_r.at[i], sibling)

    def arrived(slot, i, sems):
        return remote(part(slot, i), part(slot, i), sems.at[i], sems.at[i], partner)

    def halve(slot, i):
        for k in range(chunk):
            at = slot * OCCUPIED + i * chunk + k
            high[at], low[at] = split(win[at])

    def mark(device, c, r):
        return marks_ref[c * n * rb + device * rb + r]

    def occupied(which):
        seen, spots = 0, [0] * chunk
        for c in range(wb):
            for r in range(rb):
                hit = mark(me, c, r)
                for k in range(chunk):
                    spots[k] = jnp.where((hit == 1) & (seen == which + k), c * rb + r, spots[k])
                seen = seen + hit
        return spots

    def owned(to, rank):
        seen, row = 0, 0
        for b in range(rb):
            hit = owner_ref[me * rb + b] == to
            row = jnp.where(hit & (seen == rank), b, row)
            seen = seen + hit.astype(jnp.int32)
        return row

    @pl.loop(0, CHUNKS)
    def _(i):
        for k, spot in enumerate(occupied(i * chunk)):
            rows = slab[lax.rem(spot, rb)]
            packed[i * chunk + k] = jnp.where(spot < rb, rows[:, :blk], rows[:, blk:])
        near(i).start()
        sib(i).start()

    high[zero] = jnp.zeros((blk, blk), jnp.bfloat16)
    low[zero] = jnp.zeros((blk, blk), jnp.bfloat16)

    def note(w):
        device = lax.rem(me + w - REACH + n, n)

        seen = 0
        for c in range(wb):
            for r in range(rb):
                hit = mark(device, c, r)
                table_ref[c * span + w * rb + r] = jnp.where(hit == 1, w * OCCUPIED + seen, zero)
                seen = seen + hit

    for c in range(wb):
        table_ref[c * span + WINDOW * rb] = zero

    @pl.loop(0, CHUNKS)
    def _(i):
        arrived(4 - 4 * odd, i, near_r).wait_recv()
        far(i).start()

        @pl.when(odd == core)
        def _():
            fwd(i).start()

        for k in range(chunk):
            at = i * chunk + k
            high[REACH * OCCUPIED + at], low[REACH * OCCUPIED + at] = split(packed[at])

        @pl.when(i < WINDOW)
        def _():
            note(i)

        halve(4 - 4 * odd, i)
        arrived(3 - 2 * core, i, sib_r).wait_recv()
        halve(3 - 2 * core, i)

    @pl.loop(0, CHUNKS)
    def _(i):
        arrived(4 * odd, i, far_r).wait_recv()

        @pl.when(odd != core)
        def _():
            fwd(i).start()

        halve(4 * odd, i)

    blocks_load.wait()
    prev_load.wait()

    @pl.loop(0, CHUNKS)
    def _(i):
        arrived(1 + 2 * core, i, fwd_r).wait_recv()
        halve(1 + 2 * core, i)

    def copy(m):
        to, _ = partner_of(me, m, n)
        return remote(
            stage.at[pl.ds(m * per, per)], out_ref.at[pl.ds(me * per, per)],
            send_sem.at[m], recv_sem.at[m], to,
        )

    def arrival(m):
        _, came = partner_of(me, m, n)
        rows = out_ref.at[pl.ds(came * per, per)]
        return remote(rows, rows, send_sem.at[m], recv_sem.at[m], came)

    def compute(m, r):
        to, _ = partner_of(me, m, n)
        row = owned(to, r)
        total = None
        for pair in range(0, slots, 2):
            a_high, a_low, b_high, b_low = [], [], [], []
            for s in range(pair, min(pair + 2, slots)):
                h, l = split(blocks[row, s])
                a_high.append(h)
                a_low.append(l)
                column = column_ref[s * rb + row]
                left, right = table_ref[column], table_ref[span + column]
                b_high.append(jnp.concatenate([high[left], high[right]], axis=1))
                b_low.append(jnp.concatenate([low[left], low[right]], axis=1))
            a_high, a_low = jnp.concatenate(a_high, axis=1), jnp.concatenate(a_low, axis=1)
            b_high, b_low = jnp.concatenate(b_high, axis=0), jnp.concatenate(b_low, axis=0)
            both = jnp.dot(jnp.concatenate([a_high, a_low], axis=0), b_high, preferred_element_type=jnp.float32)
            add = both[:blk] + both[blk:] + jnp.dot(a_high, b_low, preferred_element_type=jnp.float32)
            total = add if total is None else total + add
        stage[m * per + r] = 2.0 * total - prev[row]

    @pl.loop(0, n - 1)
    def _(j):
        m = n - 1 - j
        @pl.loop(0, per)
        def _(r):
            compute(m, r)

        copy(m).start()

    @pl.loop(0, per)
    def _(r):
        compute(0, r)

    own = pltpu.make_async_copy(stage.at[pl.ds(0, per)], out_ref.at[pl.ds(me * per, per)], load_sem.at[3])
    own.start()

    @pl.loop(0, CHUNKS)
    def _(i):
        near(i).wait_send()
        sib(i).wait_send()
        far(i).wait_send()
        fwd(i).wait_send()

    own.wait()

    @pl.loop(0, n - 1)
    def _(j):
        m = n - 1 - j
        copy(m).wait_send()
        arrival(m).wait_recv()


def term(marks, column, owner, slab, blocks, prev, n):
    rb, _, blk, _ = blocks.shape
    width = prev.shape[2]
    count = WINDOW * OCCUPIED
    smem = pl.BlockSpec(memory_space=pltpu.SMEM)
    hbm = pl.BlockSpec(memory_space=pl.ANY)
    return pl.pallas_call(
        functools.partial(term_kernel, n),
        out_shape=jax.ShapeDtypeStruct((rb, blk, width), jnp.float32),
        in_specs=[smem] * 3 + [hbm] * 3,
        out_specs=hbm,
        scratch_shapes=[
            pltpu.VMEM(slab.shape, jnp.float32),
            pltpu.VMEM(blocks.shape, jnp.float32),
            pltpu.VMEM(prev.shape, jnp.float32),
            pltpu.VMEM((OCCUPIED, blk, blk), jnp.float32),
            pltpu.VMEM((count, blk, blk), jnp.float32),
            pltpu.VMEM((count + 1, blk, blk), jnp.bfloat16),
            pltpu.VMEM((count + 1, blk, blk), jnp.bfloat16),
            pltpu.VMEM(prev.shape, jnp.float32),
            pltpu.SMEM((width // blk * (WINDOW * rb + 1),), jnp.int32),
        ]
        + [pltpu.SemaphoreType.DMA((CHUNKS,)) for _ in range(8)]
        + [pltpu.SemaphoreType.DMA((n,))] * 2
        + [pltpu.SemaphoreType.DMA((4,))],
        compiler_params=pltpu.CompilerParams(collective_id=0, has_side_effects=True, vmem_limit_bytes=49 << 20),
    )(marks, column, owner, slab, blocks, prev)


def local(hblocks, hcols, hmask, tmask, owner, cheb_now, cheb_prev):
    n = lax.axis_size("row")
    me = lax.axis_index("row")
    rb, slots, blk, _ = hblocks.shape
    width = cheb_now.shape[1]
    relative = (hcols - (me - REACH) * rb) % (rb * n)
    column = jnp.where(hmask == 1, relative, WINDOW * rb).T.reshape(-1)
    out = term(
        tmask.T.reshape(-1), column, owner,
        cheb_now.reshape(rb, blk, width), hblocks, cheb_prev.reshape(rb, blk, width), n,
    )
    return out.reshape(rb * blk, width)


def solution(mesh):
    in_specs = (
        P(("groups", "row"), None, None, None),
        P(("groups", "row"), None),
        P(("groups", "row"), None),
        P("groups", None),
        P("groups"),
        P(("groups", "row"), None),
        P(("groups", "row"), None),
    )
    out_specs = P(("groups", "row"), None)
    return jax.shard_map(local, mesh=mesh, in_specs=in_specs, out_specs=out_specs, check_vma=False)
```
